32 devices in a mesh: groups: 2 (over y), ctg: 4 (over z), tm: 4 (over x, core).
Axes of the slice: x: 2, y: 2, z: 4, core: 2. Of those that a mesh axis runs over, the one named last changes fastest.
Arguments:
- dispatch: float32 [64, 2048], P(('groups', 'tm'), 'ctg'), parts along dimension 0, may hold values from 0 to 1
- unit_cost: float32 [64, 2048], P(('groups', 'tm'), 'ctg'), parts along dimension 0, may hold values from 0.2 to 2
- capacity: float32 [2048], P('ctg'), may hold values from 0.5 to 2
- demand: float32 [64], P(('groups', 'tm')), parts along dimension 0, may hold values from 819.2 to 1228.8
- balance_dual: float32 [64], P(('groups', 'tm')), parts along dimension 0, may hold values from -6 to 6
- ramp_dual: float32 [64, 2048], P(('groups', 'tm'), 'ctg'), parts along dimension 0, may hold values from -6 to 6
- ramp_band: int32 [2048], P('ctg'), may hold values from 1 to 8
- horizon_start: int32 [32], P('tm'), may hold values 0 or 1
- shift_factors: float32 [4096, 2048], P('ctg'), may hold values from -0.125 to 0.125
- outage_factors: float32 [32, 4096], P('ctg'), may hold values from -1 to 1
- outage_line: int32 [32], P('ctg'), may hold values from 0 to 4095
- line_limit: float32 [4096], replicated, may hold values from 0.3 to 3
- flow_dual: float32 [32, 64, 4096], P('ctg', ('groups', 'tm')), parts along dimension 1, may hold values from -1 to 1
- step_sizes: float32 [4], replicated, may hold values from 0.5 to 2
Outputs:
- new_dispatch: float32 [64, 2048], P(('groups', 'tm'), 'ctg'), parts along dimension 0
- new_flow_dual: float32 [32, 64, 4096], P('ctg', ('groups', 'tm')), parts along dimension 1
- new_balance_dual: float32 [64], P(('groups', 'tm')), parts along dimension 0
- new_ramp_dual: float32 [64, 2048], P(('groups', 'tm'), 'ctg'), parts along dimension 0
The draws below stay inside these ranges and needn't reach their ends.
There are 2 independent parts, one for each index of `groups`. The reference program is written for one: setup_inputs(seed, part) draws one part's arguments, and reference() takes and returns one part's arrays. A program takes and returns all parts, laid end to end along the dimension named above; an argument that names none is the same for every part. Nothing has to cross between parts.
All inputs are finite; a program needn't handle non-finite values. No bound on the sum of `horizon_start` on one device may be relied on, other than what follows from the above.
Results may differ from the reference program's by a relative error of at most 0.0003.
Values sent between devices are 32-bit elements; how exact they have to be, the bound alone decides.
A program may use at most 64 MiB of HBM per device.

```python
import math
import jax
import jax.numpy as jnp
from jax import lax

BUSES = 2048
LINES = 4096
CTGS = 32
INTERVALS = 32


def touch_ends(result, own_key, smallest, high):
    place = [jax.random.randint(jax.random.fold_in(own_key, axis), (), 0, length) for axis, length in enumerate(result.shape)]
    widest = result.shape.index(max(result.shape))
    neighbour = place[:widest] + [(place[widest] + 1) % result.shape[widest]] + place[widest + 1:]
    return result.at[tuple(place)].set(smallest).at[tuple(neighbour)].set(high)


def spiked(result, stream_key, source, target, shards_of, factor):
    owner, partner = [(jnp.arange(result.shape[axis_at]) // (result.shape[axis_at] // shards_of)).reshape([-1 if axis == axis_at else 1 for axis in range(result.ndim)]) for axis_at in (source, target)]
    chosen = jax.random.permutation(stream_key, shards_of)[partner]
    strong = (owner == chosen) | (owner == (partner + shards_of // 2) % shards_of)
    return jnp.where(strong, factor * result, result)


def level_of(rng, extent, cuts, smallest, high):
    loudness = 1.0
    for position, blocks in cuts:
        draws = jax.random.uniform(jax.random.fold_in(jax.random.fold_in(rng, 6), position), (blocks,), jnp.float32, smallest / len(cuts), high / len(cuts))
        loudness = loudness * jnp.repeat(jnp.exp(draws), extent[position] // blocks).reshape((-1,) + (1,) * (len(extent) - 1 - position))
    return loudness


def scatter_about(rng, extent, scale, limit, pieces=(), kind=jnp.bfloat16):
    gain = level_of(rng, extent, pieces, -0.22, 0.18) if pieces else 1.0
    entries = jax.random.normal(rng, extent, jnp.float32) * scale * gain
    return jnp.minimum(jnp.maximum(entries, -limit), limit).astype(kind)


def gaussian_with(stream_key, shape, deviation, most, pieces, heavy, kind=jnp.bfloat16):
    result = deviation * jax.random.normal(stream_key, shape, jnp.float32)
    if pieces:
        result = result * level_of(stream_key, shape, pieces, -0.22, 0.18)
    return jnp.clip(spiked(result, jax.random.fold_in(stream_key, 3), *heavy), -most, most).astype(kind)


def setup_inputs(seed: int = 0, part: int = 0) -> dict:
    keys = jax.random.split(jax.random.key(seed), 15)
    own_keys = jax.random.split(jax.random.fold_in(keys[14], part), 15)
    dispatch = jnp.clip(1.0 * jax.random.uniform(own_keys[0], (INTERVALS, BUSES), jnp.float32) ** level_of(own_keys[0], (INTERVALS, BUSES), ((0, 4), (1, 4)), -0.2, 0.2), 0.0, 1.0)
    unit_cost = jnp.clip(0.2 + 1.8 * jax.random.uniform(own_keys[1], (INTERVALS, BUSES), jnp.float32) ** level_of(own_keys[1], (INTERVALS, BUSES), ((0, 4), (1, 4)), -0.2, 0.2), 0.2, 2.0)
    capacity = jnp.clip(jnp.exp(math.log(2.0) - 1.3862944 * jax.random.uniform(keys[2], (BUSES,), jnp.float32) ** level_of(keys[2], (BUSES,), ((0, 4),), -0.2, 0.2)), 0.5, 2.0)
    demand = jnp.clip(819.2 + 409.60004 * jax.random.uniform(own_keys[3], (INTERVALS,), jnp.float32) ** level_of(own_keys[3], (INTERVALS,), ((0, 4),), -0.2, 0.2), 819.2, 1228.8)
    balance_dual = scatter_about(own_keys[4], (INTERVALS,), 1.0, 6.0, ((0, 4),), jnp.float32)
    ramp_dual = scatter_about(own_keys[5], (INTERVALS, BUSES), 0.5, 6.0, ((0, 4), (1, 4)), jnp.float32)
    ramp_band = touch_ends(jax.random.randint(keys[6], (BUSES,), 1, 9), jax.random.fold_in(keys[6], 1), 1, 8).astype(jnp.int32)
    horizon_start = touch_ends((jax.random.randint(keys[7], (INTERVALS,), 0, 6) < 1).astype(jnp.int32), jax.random.fold_in(keys[7], 1), 0, 1)
    shift_factors = scatter_about(keys[8], (LINES, BUSES), BUSES ** -0.5, 0.125, ((0, 4),), jnp.float32)
    outage_factors = jnp.clip(jax.random.uniform(keys[9], (CTGS, LINES), jnp.float32, -1.0, 1.0) * level_of(keys[9], (CTGS, LINES), ((0, 4),), -0.4, 0.0), -1.0, 1.0)
    outage_line = touch_ends(jax.random.randint(keys[10], (CTGS,), 0, LINES), jax.random.fold_in(keys[10], 1), 0, LINES - 1).astype(jnp.int32)
    line_limit = jnp.clip(jnp.exp(jax.random.uniform(keys[11], (LINES,), jnp.float32, math.log(0.3), math.log(3.0))), 0.3, 3.0)
    flow_dual = gaussian_with(own_keys[12], (CTGS, INTERVALS, LINES), 0.05, 1.0, ((0, 4), (1, 4)), (0, 2, 4, 2.0), jnp.float32)
    step_sizes = jnp.clip(jnp.exp(jax.random.uniform(keys[13], (4,), jnp.float32, math.log(0.5), math.log(2.0))), 0.5, 2.0)
    return dict(dispatch=dispatch, unit_cost=unit_cost, capacity=capacity, demand=demand, balance_dual=balance_dual, ramp_dual=ramp_dual, ramp_band=ramp_band, horizon_start=horizon_start, shift_factors=shift_factors, outage_factors=outage_factors, outage_line=outage_line, line_limit=line_limit, flow_dual=flow_dual, step_sizes=step_sizes)


highest = lax.Precision.HIGHEST


def effective_column(column, line):
    positions = jnp.arange(column.shape[0], dtype=jnp.int32)
    return jnp.where(positions == line, -jnp.ones_like(column), column)


def dual_update(value, step, bound):
    return value - step * jnp.clip(value / step, -bound, bound)


def reference(dispatch, unit_cost, capacity, demand, balance_dual, ramp_dual, ramp_band, horizon_start, shift_factors, outage_factors, outage_line, line_limit, flow_dual, step_sizes):
    primal_step = 0.1 * step_sizes[0]
    flow_step = step_sizes[1]
    balance_step = step_sizes[2] / BUSES
    ramp_step = step_sizes[3]
    times = jnp.arange(INTERVALS, dtype=jnp.int32)
    coupled = jnp.where((times > 0) & (horizon_start == 0), 1.0, 0.0).astype(dispatch.dtype)
    ramp_limit = 0.05 * ramp_band.astype(dispatch.dtype)
    positions = jnp.arange(LINES, dtype=jnp.int32)

    def accumulate(total, item):
        duals, column, line = item
        column = effective_column(column, line)
        product = jnp.dot(duals, column, precision=highest)
        marker = (positions == line).astype(dispatch.dtype)
        return total + duals + product[:, None] * marker[None, :], None

    adjoint, unused = lax.scan(accumulate, jnp.zeros((INTERVALS, LINES), dispatch.dtype), (flow_dual, outage_factors, outage_line))
    weighted = ramp_dual * coupled[:, None]
    following = jnp.concatenate([weighted[1:], jnp.zeros_like(weighted[:1])], 0)
    gradient = unit_cost + balance_dual[:, None] + jnp.dot(adjoint, shift_factors, precision=highest) + weighted - following
    new_dispatch = jnp.clip(dispatch - primal_step * gradient, 0.0, capacity[None, :])
    extended = 2.0 * new_dispatch - dispatch
    base = jnp.dot(extended, shift_factors.T, precision=highest)

    def update(item):
        duals, column, line = item
        column = effective_column(column, line)
        outflow = lax.dynamic_slice_in_dim(base, line, 1, 1)[:, 0]
        flow = base + column[None, :] * outflow[:, None]
        return dual_update(duals + flow_step * flow, flow_step, line_limit[None, :])

    new_flow_dual = lax.map(update, (flow_dual, outage_factors, outage_line))
    new_balance_dual = balance_dual + balance_step * (jnp.sum(extended, 1) - demand)
    previous = jnp.concatenate([jnp.zeros_like(extended[:1]), extended[:-1]], 0)
    ramp_value = ramp_dual + ramp_step * (extended - previous)
    new_ramp_dual = coupled[:, None] * dual_update(ramp_value, ramp_step, ramp_limit[None, :])
    return new_dispatch, new_flow_dual, new_balance_dual, new_ramp_dual
```

```python
import functools
import jax
import jax.numpy as jnp
from jax import lax
from jax.experimental import pallas as pl
from jax.experimental.pallas import tpu as pltpu
from jax.sharding import PartitionSpec as P

BUSES = 2048


highest = lax.Precision.HIGHEST


def from_behind(block, axis, distance):
    devices = range(lax.axis_size(axis))
    route = [(i - distance, i) for i in devices if i - distance in devices]
    return lax.ppermute(block, axis, route)


def dual_update(value, step, bound):
    return value - step * jnp.clip(value / step, -bound, bound)


def local(
    dispatch,
    unit_cost,
    capacity,
    demand,
    balance_dual,
    ramp_dual,
    ramp_band,
    horizon_start,
    shift_factors,
    outage_factors,
    outage_line,
    line_limit,
    flow_dual,
    step_sizes,
):
    count_times = dispatch.shape[0]
    total_lines = outage_factors.shape[1]
    primal_step = 0.1 * step_sizes[0]
    flow_step = step_sizes[1]
    balance_step = step_sizes[2] / BUSES
    ramp_step = step_sizes[3]
    first_time = lax.axis_index("tm") * count_times
    times = first_time + jnp.arange(count_times, dtype=jnp.int32)
    coupled = jnp.where((times > 0) & (horizon_start == 0), 1.0, 0.0).astype(jnp.float32)
    ramp_limit = 0.05 * ramp_band.astype(jnp.float32)
    positions = jnp.arange(total_lines, dtype=jnp.int32)
    is_outage = positions[None, :] == outage_line[:, None]
    column = jnp.where(is_outage, -1.0, outage_factors)
    marker = is_outage.astype(jnp.float32)
    product = jnp.einsum("ctl,cl->ct", flow_dual, column, precision=highest)
    adjoint = jnp.sum(flow_dual, 0) + jnp.einsum("ct,cl->tl", product, marker, precision=highest)
    line_part = lax.psum_scatter(adjoint, "ctg", scatter_dimension=1, tiled=True)
    partial_bus = jnp.dot(line_part, shift_factors, precision=highest)
    bus_part = lax.psum_scatter(partial_bus, "ctg", scatter_dimension=1, tiled=True)
    weighted = ramp_dual * coupled[:, None]
    incoming = from_behind(weighted[:1], "tm", -1)
    following = jnp.concatenate([weighted[1:], incoming], 0)
    gradient = unit_cost + balance_dual[:, None] + bus_part + weighted - following
    new_dispatch = jnp.clip(dispatch - primal_step * gradient, 0.0, capacity[None, :])
    extended = 2.0 * new_dispatch - dispatch
    base_mine = jnp.dot(
        lax.all_gather(extended, "ctg", axis=1, tiled=True), shift_factors.T, precision=highest
    )
    total = lax.psum(jnp.sum(extended, 1), "ctg")
    base = lax.all_gather(base_mine, "ctg", axis=1, tiled=True)
    outflow = jnp.einsum("tl,cl->ct", base, marker, precision=highest)
    flow = base[None, :, :] + column[:, None, :] * outflow[:, :, None]
    new_flow_dual = dual_update(flow_dual + flow_step * flow, flow_step, line_limit[None, None, :])
    new_balance_dual = balance_dual + balance_step * (total - demand)
    previous = from_behind(extended[-1:], "tm", 1)
    before = jnp.concatenate([previous, extended[:-1]], 0)
    ramp_value = ramp_dual + ramp_step * (extended - before)
    new_ramp_dual = coupled[:, None] * dual_update(ramp_value, ramp_step, ramp_limit[None, :])
    return (new_dispatch, new_flow_dual, new_balance_dual, new_ramp_dual)


MESH = pl.DeviceIdType.MESH
LANES = 128


def partner(me, k):
    if k == 3:
        return 3 - me
    if k == 2:
        return lax.rem(me + 2, 4)
    return me + 1 - 2 * lax.rem(me, 2)


def column_of(scalars, rows, dtype):
    place = lax.broadcasted_iota(jnp.int32, (rows, 1), 0)
    result = jnp.zeros((rows, 1), dtype)
    for i in range(rows):
        result = jnp.where(place == i, scalars[i], result)
    return result


def split(x):
    high = x.astype(jnp.bfloat16)
    low = (x - high.astype(jnp.float32)).astype(jnp.bfloat16)
    return high, low


def times(x, high, low, axis):
    rows = x.shape[0]
    both = jnp.concatenate(split(x), 0)
    dims = (((1,), (axis,)), ((), ()))
    a = lax.dot_general(both, high, dims, preferred_element_type=jnp.float32)
    b = lax.dot_general(both, low, dims, preferred_element_type=jnp.float32)
    c = a + b
    return c[:rows] + c[rows:]


def kernel(
    buses,
    demand,
    balance_dual,
    horizon_start,
    outage_line,
    step_sizes,
    dispatch_in,
    unit_cost_in,
    capacity_in,
    ramp_dual_in,
    ramp_band_in,
    shift_in,
    outage_in,
    limit_in,
    flow_in,
    new_dispatch,
    new_flow,
    new_balance,
    new_ramp,
    dispatch,
    unit_cost,
    capacity,
    ramp_dual,
    ramp_band,
    shift,
    column,
    limit,
    flow,
    high,
    low,
    adjoint,
    adjoint_got,
    bus,
    bus_got,
    extended_all,
    base_all,
    row_out,
    row_in,
    last_out,
    last_in,
    load_sem,
    shift_sem,
    send_sem,
    recv_sem,
    row_send,
    row_recv,
):
    me = lax.axis_index("ctg")
    tm = lax.axis_index("tm")
    tms = lax.axis_size("tm")
    ctgs, rows, lines = flow.shape
    mine_lines = lines // 4
    mine_buses = buses // 4
    f32 = jnp.float32
    after = lax.rem(tm + 1, tms)
    ahead = lax.rem(tm + tms - 1, tms)

    loads = [
        pltpu.make_async_copy(a, b, load_sem.at[i])
        for i, (a, b) in enumerate(
            [
                (flow_in, flow),
                (outage_in, column),
                (ramp_dual_in, ramp_dual),
                (dispatch_in, dispatch),
                (unit_cost_in, unit_cost),
                (capacity_in, capacity),
                (ramp_band_in, ramp_band),
                (limit_in, limit),
            ]
        )
    ]
    for load in loads:
        load.start()
    pieces = shift_sem.shape[0]
    depth = mine_lines // pieces

    def piece(i):
        there = pl.ds(pl.multiple_of(i * depth, depth), depth)
        return pltpu.make_async_copy(shift_in.at[there], shift.at[there], shift_sem.at[i])

    for i in range(pieces):
        piece(i).start()

    barrier = pltpu.get_barrier_semaphore()
    for k in (3, 2, 1):
        pl.semaphore_signal(barrier, inc=1, device_id={"ctg": partner(me, k)}, device_id_type=MESH)
    for t in (after, ahead):
        pl.semaphore_signal(barrier, inc=1, device_id={"tm": t}, device_id_type=MESH)

    primal_step = 0.1 * step_sizes[0]
    flow_step = step_sizes[1]
    balance_step = step_sizes[2] / buses
    ramp_step = step_sizes[3]
    starts = column_of(horizon_start, rows, jnp.int32)
    time = tm * rows + lax.broadcasted_iota(jnp.int32, (rows, 1), 0)
    coupled = jnp.where((time > 0) & (starts == 0), 1.0, 0.0).astype(f32)
    balance = column_of(balance_dual, rows, f32)
    lane = lax.broadcasted_iota(jnp.int32, (rows, LANES), 1)
    line_of = column_of(outage_line, ctgs, jnp.int32)

    loads[1].wait()
    position = lax.broadcasted_iota(jnp.int32, (ctgs, lines), 1)
    column[...] = jnp.where(position == line_of, -1.0, column[...])
    loads[0].wait()

    def gather_product(k, sums):
        here = pl.ds(pl.multiple_of(k * LANES, LANES), LANES)
        total = jnp.zeros((rows, LANES), f32)
        result = []
        for c in range(ctgs):
            duals = flow[c, :, here]
            total = total + duals
            result.append(sums[c] + duals * column[c : c + 1, here])
        adjoint[:, here] = total
        return tuple(result)

    zeros = tuple(jnp.zeros((rows, LANES), f32) for c in range(ctgs))
    sums = lax.fori_loop(0, lines // LANES, gather_product, zeros, unroll=4)
    product = [jnp.sum(s, 1, keepdims=True) for s in sums]

    def add_product(k, unused):
        here = pl.ds(pl.multiple_of(k * LANES, LANES), LANES)
        total = adjoint[:, here]
        for c in range(ctgs):
            total = total + jnp.where(lane == outage_line[c] - k * LANES, product[c], 0.0)
        adjoint[:, here] = total
        return unused

    lax.fori_loop(0, lines // LANES, add_product, 0, unroll=4)

    def to_partner(phase, k, source, target):
        return pltpu.make_async_remote_copy(
            src_ref=source,
            dst_ref=target,
            send_sem=send_sem.at[phase, k - 1],
            recv_sem=recv_sem.at[phase, k - 1],
            device_id={"ctg": partner(me, k)},
            device_id_type=MESH,
        )

    def span(i, width):
        return pl.ds(pl.multiple_of(i * width, width), width)

    pl.semaphore_wait(barrier, 5)
    first = {}
    for k in (3, 2, 1):
        first[k] = to_partner(0, k, adjoint.at[:, span(partner(me, k), mine_lines)], adjoint_got.at[k - 1])
        first[k].start()
    loads[2].wait()
    weighted = ramp_dual[...] * coupled
    row_out[...] = weighted[:1]
    row_copy = pltpu.make_async_remote_copy(
        src_ref=row_out, dst_ref=row_in, send_sem=row_send.at[0], recv_sem=row_recv.at[0],
        device_id={"tm": ahead}, device_id_type=MESH)
    row_copy.start()

    @pl.loop(0, pieces)
    def _(i):
        piece(i).wait()

        @pl.loop(0, depth // 16)
        def _(r):
            there = pl.ds(pl.multiple_of(i * depth + r * 16, 16), 16)
            a, b = split(shift[there])
            high[there] = a
            low[there] = b

    for load in loads[3:]:
        load.wait()

    line_part = adjoint[:, span(me, mine_lines)]
    for k in (1, 2, 3):
        first[k].wait_recv()
        line_part = line_part + adjoint_got[k - 1]

    second = {}
    for k in (3, 2, 1, 0):
        owner = partner(me, k) if k else me
        there = span(owner, mine_buses)
        part = times(line_part, high[:, there], low[:, there], 0)
        if k:
            bus[k - 1] = part
            second[k] = to_partner(1, k, bus.at[k - 1], bus_got.at[k - 1])
            second[k].start()
    bus_part = part
    row_copy.wait_recv()
    sub = lax.broadcasted_iota(jnp.int32, (rows, mine_buses), 0)
    incoming = jnp.where(tm == tms - 1, 0.0, row_in[...])
    following = jnp.where(sub == rows - 1, incoming, jnp.roll(weighted, -1, 0))
    known = unit_cost[...] + balance + weighted - following
    for k in (1, 2, 3):
        second[k].wait_recv()
        bus_part = bus_part + bus_got[k - 1]
    gradient = known + bus_part
    fresh = jnp.minimum(jnp.maximum(dispatch[...] - primal_step * gradient, 0.0), capacity[...])
    extended = 2.0 * fresh - dispatch[...]
    extended_all[me] = extended
    third = {}
    for k in (3, 2, 1):
        third[k] = to_partner(2, k, extended_all.at[me], extended_all.at[me])
        third[k].start()
    last_out[...] = extended[rows - 1 :]
    last_copy = pltpu.make_async_remote_copy(
        src_ref=last_out, dst_ref=last_in, send_sem=row_send.at[1], recv_sem=row_recv.at[1],
        device_id={"tm": after}, device_id_type=MESH)
    last_copy.start()
    new_dispatch[...] = fresh

    total = jnp.sum(extended, 1, keepdims=True)
    base = None
    for k in (0, 1, 2, 3):
        if k:
            third[k].wait_recv()
        owner = partner(me, k) if k else me
        block = extended_all[owner]
        there = span(owner, mine_buses)
        if k:
            total = total + jnp.sum(block, 1, keepdims=True)
        part = times(block, high[:, there], low[:, there], 1)
        base = part if base is None else base + part
    base_all[me] = base
    fourth = {}
    for k in (3, 2, 1):
        fourth[k] = to_partner(3, k, base_all.at[me], base_all.at[me])
        fourth[k].start()

    wanted = column_of(demand, rows, f32)
    settled = balance + balance_step * (total - wanted)
    eye = lax.broadcasted_iota(jnp.int32, (rows, rows), 0) == lax.broadcasted_iota(jnp.int32, (rows, rows), 1)
    new_balance[...] = jnp.sum(jnp.where(eye, settled, 0.0), 0, keepdims=True)
    last_copy.wait_recv()
    previous = jnp.where(tm == 0, 0.0, last_in[...])
    before = jnp.where(sub == 0, previous, jnp.roll(extended, 1, 0))
    ramp_value = ramp_dual[...] + ramp_step * (extended - before)
    band = ramp_step * (0.05 * ramp_band[...].astype(f32))
    new_ramp[...] = coupled * (ramp_value - jnp.minimum(jnp.maximum(ramp_value, -band), band))

    for k in (1, 2, 3):
        fourth[k].wait_recv()
    tiles = mine_lines // LANES

    def pick(k, found):
        j = k // tiles
        here = pl.ds(pl.multiple_of((k - j * tiles) * LANES, LANES), LANES)
        block = base_all[j, :, here]
        return tuple(
            found[c] + jnp.where(lane == outage_line[c] - k * LANES, block, 0.0) for c in range(ctgs)
        )

    found = lax.fori_loop(0, lines // LANES, pick, zeros, unroll=4)
    outflow = [flow_step * jnp.sum(f, 1, keepdims=True) for f in found]

    def update(k, unused):
        j = k // tiles
        here = pl.ds(pl.multiple_of(k * LANES, LANES), LANES)
        inner = pl.ds(pl.multiple_of((k - j * tiles) * LANES, LANES), LANES)
        shared = flow_step * base_all[j, :, inner]
        bound = flow_step * limit[:, here]
        for c in range(ctgs):
            value = flow[c, :, here] + (shared + column[c : c + 1, here] * outflow[c])
            new_flow[c, :, here] = value - jnp.minimum(jnp.maximum(value, -bound), bound)
        return unused

    lax.fori_loop(0, lines // LANES, update, 0, unroll=4)

    for group in (first, second, third, fourth):
        for k in (1, 2, 3):
            group[k].wait_send()
    row_copy.wait_send()
    last_copy.wait_send()


def fused(
    dispatch,
    unit_cost,
    capacity,
    demand,
    balance_dual,
    ramp_dual,
    ramp_band,
    horizon_start,
    shift_factors,
    outage_factors,
    outage_line,
    line_limit,
    flow_dual,
    step_sizes,
):
    f32 = jnp.float32
    rows, own = dispatch.shape
    ctgs, unused, lines = flow_dual.shape
    buses = shift_factors.shape[1]
    line_block = lines // 4
    smem = pl.BlockSpec(memory_space=pltpu.SMEM)
    vmem = pl.BlockSpec(memory_space=pltpu.VMEM)
    anywhere = pl.BlockSpec(memory_space=pl.ANY)
    hbm = pl.BlockSpec(memory_space=pltpu.HBM)
    outs = pl.pallas_call(
        functools.partial(kernel, buses),
        out_shape=(
            jax.ShapeDtypeStruct((rows, own), f32),
            jax.ShapeDtypeStruct(flow_dual.shape, f32),
            jax.ShapeDtypeStruct((1, rows), f32),
            jax.ShapeDtypeStruct((rows, own), f32),
        ),
        in_specs=[smem] * 5 + [hbm] * 9,
        out_specs=[vmem] * 4,
        scratch_shapes=[
            pltpu.VMEM((rows, own), f32),
            pltpu.VMEM((rows, own), f32),
            pltpu.VMEM((1, own), f32),
            pltpu.VMEM((rows, own), f32),
            pltpu.VMEM((1, own), jnp.int32),
            pltpu.VMEM(shift_factors.shape, f32),
            pltpu.VMEM(outage_factors.shape, f32),
            pltpu.VMEM((1, lines), f32),
            pltpu.VMEM(flow_dual.shape, f32),
            pltpu.VMEM(shift_factors.shape, jnp.bfloat16),
            pltpu.VMEM(shift_factors.shape, jnp.bfloat16),
            pltpu.VMEM((rows, lines), f32),
            pltpu.VMEM((3, rows, line_block), f32),
            pltpu.VMEM((3, rows, own), f32),
            pltpu.VMEM((3, rows, own), f32),
            pltpu.VMEM((4, rows, own), f32),
            pltpu.VMEM((4, rows, line_block), f32),
            pltpu.VMEM((1, own), f32),
            pltpu.VMEM((1, own), f32),
            pltpu.VMEM((1, own), f32),
            pltpu.VMEM((1, own), f32),
            pltpu.SemaphoreType.DMA((8,)),
            pltpu.SemaphoreType.DMA((8,)),
            pltpu.SemaphoreType.DMA((4, 3)),
            pltpu.SemaphoreType.DMA((4, 3)),
            pltpu.SemaphoreType.DMA((2,)),
            pltpu.SemaphoreType.DMA((2,)),
        ],
        compiler_params=pltpu.CompilerParams(
            collective_id=0, has_side_effects=True, vmem_limit_bytes=40 * 2**20
        ),
    )(
        demand,
        balance_dual,
        horizon_start,
        outage_line,
        step_sizes,
        dispatch,
        unit_cost,
        capacity.reshape(1, own),
        ramp_dual,
        ramp_band.reshape(1, own),
        shift_factors,
        outage_factors,
        line_limit.reshape(1, lines),
        flow_dual,
    )
    return outs[0], outs[1], outs[2].reshape(rows), outs[3]


def choose(*blocks):
    rows, own = blocks[0].shape
    lines = blocks[9].shape[1]
    whole = rows == 8 and own % LANES == 0 and lines % (4 * LANES) == 0
    if lax.axis_size("ctg") == 4 and lax.axis_size("tm") > 2 and whole:
        return fused(*blocks)
    return local(*blocks)


def solution(mesh):
    in_specs = (
        P(("groups", "tm"), "ctg"),
        P(("groups", "tm"), "ctg"),
        P("ctg"),
        P(("groups", "tm")),
        P(("groups", "tm")),
        P(("groups", "tm"), "ctg"),
        P("ctg"),
        P("tm"),
        P("ctg", None),
        P("ctg", None),
        P("ctg"),
        P(),
        P("ctg", ("groups", "tm"), None),
        P(),
    )
    out_specs = (
        P(("groups", "tm"), "ctg"),
        P("ctg", ("groups", "tm"), None),
        P(("groups", "tm")),
        P(("groups", "tm"), "ctg"),
    )
    return jax.shard_map(choose, mesh=mesh, in_specs=in_specs, out_specs=out_specs, check_vma=False)
```

```python
import functools
import jax
import jax.numpy as jnp
from jax import lax
from jax.experimental import pallas as pl
from jax.experimental.pallas import tpu as pltpu
from jax.sharding import PartitionSpec as P

BUSES = 2048


highest = lax.Precision.HIGHEST


def from_behind(block, axis, distance):
    devices = range(lax.axis_size(axis))
    route = [(i - distance, i) for i in devices if i - distance in devices]
    return lax.ppermute(block, axis, route)


def dual_update(value, step, bound):
    return value - step * jnp.clip(value / step, -bound, bound)


def local(
    dispatch,
    unit_cost,
    capacity,
    demand,
    balance_dual,
    ramp_dual,
    ramp_band,
    horizon_start,
    shift_factors,
    outage_factors,
    outage_line,
    line_limit,
    flow_dual,
    step_sizes,
):
    count_times = dispatch.shape[0]
    total_lines = outage_factors.shape[1]
    primal_step = 0.1 * step_sizes[0]
    flow_step = step_sizes[1]
    balance_step = step_sizes[2] / BUSES
    ramp_step = step_sizes[3]
    first_time = lax.axis_index("tm") * count_times
    times = first_time + jnp.arange(count_times, dtype=jnp.int32)
    coupled = jnp.where((times > 0) & (horizon_start == 0), 1.0, 0.0).astype(jnp.float32)
    ramp_limit = 0.05 * ramp_band.astype(jnp.float32)
    positions = jnp.arange(total_lines, dtype=jnp.int32)
    is_outage = positions[None, :] == outage_line[:, None]
    column = jnp.where(is_outage, -1.0, outage_factors)
    marker = is_outage.astype(jnp.float32)
    product = jnp.einsum("ctl,cl->ct", flow_dual, column, precision=highest)
    adjoint = jnp.sum(flow_dual, 0) + jnp.einsum("ct,cl->tl", product, marker, precision=highest)
    line_part = lax.psum_scatter(adjoint, "ctg", scatter_dimension=1, tiled=True)
    partial_bus = jnp.dot(line_part, shift_factors, precision=highest)
    bus_part = lax.psum_scatter(partial_bus, "ctg", scatter_dimension=1, tiled=True)
    weighted = ramp_dual * coupled[:, None]
    incoming = from_behind(weighted[:1], "tm", -1)
    following = jnp.concatenate([weighted[1:], incoming], 0)
    gradient = unit_cost + balance_dual[:, None] + bus_part + weighted - following
    new_dispatch = jnp.clip(dispatch - primal_step * gradient, 0.0, capacity[None, :])
    extended = 2.0 * new_dispatch - dispatch
    base_mine = jnp.dot(
        lax.all_gather(extended, "ctg", axis=1, tiled=True), shift_factors.T, precision=highest
    )
    total = lax.psum(jnp.sum(extended, 1), "ctg")
    base = lax.all_gather(base_mine, "ctg", axis=1, tiled=True)
    outflow = jnp.einsum("tl,cl->ct", base, marker, precision=highest)
    flow = base[None, :, :] + column[:, None, :] * outflow[:, :, None]
    new_flow_dual = dual_update(flow_dual + flow_step * flow, flow_step, line_limit[None, None, :])
    new_balance_dual = balance_dual + balance_step * (total - demand)
    previous = from_behind(extended[-1:], "tm", 1)
    before = jnp.concatenate([previous, extended[:-1]], 0)
    ramp_value = ramp_dual + ramp_step * (extended - before)
    new_ramp_dual = coupled[:, None] * dual_update(ramp_value, ramp_step, ramp_limit[None, :])
    return (new_dispatch, new_flow_dual, new_balance_dual, new_ramp_dual)


MESH = pl.DeviceIdType.MESH
LANES = 128


def partner(me, k):
    if k == 3:
        return 3 - me
    if k == 2:
        return lax.rem(me + 2, 4)
    return me + 1 - 2 * lax.rem(me, 2)


def column_of(scalars, rows, dtype):
    place = lax.broadcasted_iota(jnp.int32, (rows, 1), 0)
    result = jnp.zeros((rows, 1), dtype)
    for i in range(rows):
        result = jnp.where(place == i, scalars[i], result)
    return result


def split(x):
    high = x.astype(jnp.bfloat16)
    low = (x - high.astype(jnp.float32)).astype(jnp.bfloat16)
    return high, low


def times(x, high, low, axis):
    rows = x.shape[0]
    both = jnp.concatenate(split(x), 0)
    dims = (((1,), (axis,)), ((), ()))
    a = lax.dot_general(both, high, dims, preferred_element_type=jnp.float32)
    b = lax.dot_general(both, low, dims, preferred_element_type=jnp.float32)
    c = a + b
    return c[:rows] + c[rows:]


def kernel(
    buses,
    demand_in,
    balance_in,
    start_in,
    outage_line_in,
    step_in,
    dispatch_in,
    unit_cost_in,
    capacity_in,
    ramp_dual_in,
    ramp_band_in,
    shift_in,
    outage_in,
    flow_in,
    dispatch_to,
    base_to,
    balance_to,
    ramp_to,
    demand,
    balance_dual,
    horizon_start,
    outage_line,
    step_sizes,
    new_dispatch,
    new_balance,
    new_ramp,
    dispatch,
    unit_cost,
    capacity,
    ramp_dual,
    ramp_band,
    shift,
    column,
    flow,
    high,
    low,
    adjoint,
    adjoint_got,
    bus,
    bus_got,
    extended_all,
    base_all,
    row_out,
    row_in,
    last_out,
    last_in,
    load_sem,
    store_sem,
    shift_sem,
    send_sem,
    recv_sem,
    row_send,
    row_recv,
):
    me = lax.axis_index("ctg")
    tm = lax.axis_index("tm")
    tms = lax.axis_size("tm")
    ctgs, rows, lines = flow.shape
    mine_lines = lines // 4
    mine_buses = buses // 4
    f32 = jnp.float32
    after = lax.rem(tm + 1, tms)
    ahead = lax.rem(tm + tms - 1, tms)

    barrier = pltpu.get_barrier_semaphore()
    for k in (3, 2, 1):
        pl.semaphore_signal(barrier, inc=1, device_id={"ctg": partner(me, k)}, device_id_type=MESH)
    for t in (after, ahead):
        pl.semaphore_signal(barrier, inc=1, device_id={"tm": t}, device_id_type=MESH)

    loads = [
        pltpu.make_async_copy(a, b, load_sem.at[i])
        for i, (a, b) in enumerate(
            [
                (flow_in, flow),
                (outage_in, column),
                (ramp_dual_in, ramp_dual),
                (dispatch_in, dispatch),
                (unit_cost_in, unit_cost),
                (capacity_in, capacity),
                (ramp_band_in, ramp_band),
                (outage_line_in, outage_line),
                (step_in, step_sizes),
                (start_in, horizon_start),
                (balance_in, balance_dual),
                (demand_in, demand),
            ]
        )
    ]
    for load in loads:
        load.start()
    pieces = shift_sem.shape[0]
    depth = mine_lines // pieces

    def piece(i):
        there = pl.ds(pl.multiple_of(i * depth, depth), depth)
        return pltpu.make_async_copy(shift_in.at[there], shift.at[there], shift_sem.at[i])

    for i in range(pieces):
        piece(i).start()

    for load in loads[7:]:
        load.wait()
    primal_step = 0.1 * step_sizes[0]
    flow_step = step_sizes[1]
    balance_step = step_sizes[2] / buses
    ramp_step = step_sizes[3]
    starts = column_of(horizon_start, rows, jnp.int32)
    time = tm * rows + lax.broadcasted_iota(jnp.int32, (rows, 1), 0)
    coupled = jnp.where((time > 0) & (starts == 0), 1.0, 0.0).astype(f32)
    balance = column_of(balance_dual, rows, f32)
    lane = lax.broadcasted_iota(jnp.int32, (rows, LANES), 1)
    line_of = column_of(outage_line, ctgs, jnp.int32)

    loads[1].wait()
    position = lax.broadcasted_iota(jnp.int32, (ctgs, lines), 1)
    column[...] = jnp.where(position == line_of, -1.0, column[...])
    loads[0].wait()

    def gather_product(k, sums):
        here = pl.ds(pl.multiple_of(k * LANES, LANES), LANES)
        total = jnp.zeros((rows, LANES), f32)
        result = []
        for c in range(ctgs):
            duals = flow[c, :, here]
            total = total + duals
            result.append(sums[c] + duals * column[c : c + 1, here])
        adjoint[:, here] = total
        return tuple(result)

    zeros = tuple(jnp.zeros((rows, LANES), f32) for c in range(ctgs))
    sums = lax.fori_loop(0, lines // LANES, gather_product, zeros, unroll=4)
    product = [jnp.sum(s, 1, keepdims=True) for s in sums]

    def add_product(k, unused):
        here = pl.ds(pl.multiple_of(k * LANES, LANES), LANES)
        total = adjoint[:, here]
        for c in range(ctgs):
            total = total + jnp.where(lane == outage_line[c] - k * LANES, product[c], 0.0)
        adjoint[:, here] = total
        return unused

    lax.fori_loop(0, lines // LANES, add_product, 0, unroll=4)

    def to_partner(phase, k, source, target):
        return pltpu.make_async_remote_copy(
            src_ref=source,
            dst_ref=target,
            send_sem=send_sem.at[phase, k - 1],
            recv_sem=recv_sem.at[phase, k - 1],
            device_id={"ctg": partner(me, k)},
            device_id_type=MESH,
        )

    def span(i, width):
        return pl.ds(pl.multiple_of(i * width, width), width)

    pl.semaphore_wait(barrier, 5)
    first = {}
    for k in (3, 2, 1):
        first[k] = to_partner(0, k, adjoint.at[:, span(partner(me, k), mine_lines)], adjoint_got.at[k - 1])
        first[k].start()
    loads[2].wait()
    weighted = ramp_dual[...] * coupled
    row_out[...] = weighted[:1]
    row_copy = pltpu.make_async_remote_copy(
        src_ref=row_out, dst_ref=row_in, send_sem=row_send.at[0], recv_sem=row_recv.at[0],
        device_id={"tm": ahead}, device_id_type=MESH)
    row_copy.start()

    @pl.loop(0, pieces)
    def _(i):
        piece(i).wait()

        @pl.loop(0, depth // 16)
        def _(r):
            there = pl.ds(pl.multiple_of(i * depth + r * 16, 16), 16)
            a, b = split(shift[there])
            high[there] = a
            low[there] = b

    for load in loads[3:7]:
        load.wait()

    line_part = adjoint[:, span(me, mine_lines)]
    for k in (1, 2, 3):
        first[k].wait_recv()
        line_part = line_part + adjoint_got[k - 1]

    second = {}
    for k in (3, 2, 1, 0):
        owner = partner(me, k) if k else me
        there = span(owner, mine_buses)
        part = times(line_part, high[:, there], low[:, there], 0)
        if k:
            bus[k - 1] = part
            second[k] = to_partner(1, k, bus.at[k - 1], bus_got.at[k - 1])
            second[k].start()
    bus_part = part
    row_copy.wait_recv()
    sub = lax.broadcasted_iota(jnp.int32, (rows, mine_buses), 0)
    incoming = jnp.where(tm == tms - 1, 0.0, row_in[...])
    following = jnp.where(sub == rows - 1, incoming, jnp.roll(weighted, -1, 0))
    known = unit_cost[...] + balance + weighted - following
    for k in (1, 2, 3):
        second[k].wait_recv()
        bus_part = bus_part + bus_got[k - 1]
    gradient = known + bus_part
    fresh = jnp.minimum(jnp.maximum(dispatch[...] - primal_step * gradient, 0.0), capacity[...])
    extended = 2.0 * fresh - dispatch[...]
    extended_all[me] = extended
    third = {}
    for k in (3, 2, 1):
        third[k] = to_partner(2, k, extended_all.at[me], extended_all.at[me])
        third[k].start()
    last_out[...] = extended[rows - 1 :]
    last_copy = pltpu.make_async_remote_copy(
        src_ref=last_out, dst_ref=last_in, send_sem=row_send.at[1], recv_sem=row_recv.at[1],
        device_id={"tm": after}, device_id_type=MESH)
    last_copy.start()
    new_dispatch[...] = fresh
    stores = [pltpu.make_async_copy(new_dispatch, dispatch_to, store_sem.at[0])]
    stores[0].start()

    total = jnp.sum(extended, 1, keepdims=True)
    base = None
    for k in (0, 1, 2, 3):
        if k:
            third[k].wait_recv()
        owner = partner(me, k) if k else me
        block = extended_all[owner]
        there = span(owner, mine_buses)
        if k:
            total = total + jnp.sum(block, 1, keepdims=True)
        part = times(block, high[:, there], low[:, there], 1)
        base = part if base is None else base + part
    base_all[me] = base
    fourth = {}
    for k in (3, 2, 1):
        fourth[k] = to_partner(3, k, base_all.at[me], base_all.at[me])
        fourth[k].start()

    wanted = column_of(demand, rows, f32)
    settled = balance + balance_step * (total - wanted)
    eye = lax.broadcasted_iota(jnp.int32, (rows, rows), 0) == lax.broadcasted_iota(jnp.int32, (rows, rows), 1)
    new_balance[...] = jnp.sum(jnp.where(eye, settled, 0.0), 0, keepdims=True)
    last_copy.wait_recv()
    previous = jnp.where(tm == 0, 0.0, last_in[...])
    before = jnp.where(sub == 0, previous, jnp.roll(extended, 1, 0))
    ramp_value = ramp_dual[...] + ramp_step * (extended - before)
    band = ramp_step * (0.05 * ramp_band[...].astype(f32))
    new_ramp[...] = coupled * (ramp_value - jnp.minimum(jnp.maximum(ramp_value, -band), band))
    stores.append(pltpu.make_async_copy(new_balance, balance_to, store_sem.at[1]))
    stores.append(pltpu.make_async_copy(new_ramp, ramp_to, store_sem.at[2]))
    stores[1].start()
    stores[2].start()

    for k in (0, 1, 2, 3):
        if k:
            fourth[k].wait_recv()
        owner = partner(me, k) if k else me
        stores.append(pltpu.make_async_copy(base_all.at[owner], base_to.at[owner], store_sem.at[3 + k]))
        stores[-1].start()

    for group in (first, second, third, fourth):
        for k in (1, 2, 3):
            group[k].wait_send()
    row_copy.wait_send()
    last_copy.wait_send()
    for store in stores:
        store.wait()


def finish(
    fresh_in,
    base_in,
    balance_in,
    ramp_in,
    outage_in,
    outage_line_in,
    limit_in,
    flow_in,
    step_in,
    fresh_to,
    flow_to,
    balance_to,
    ramp_to,
    fresh,
    base,
    balance,
    ramp,
    column,
    outage_line,
    limit,
    flow,
    step_sizes,
    new_flow,
    sem,
    flow_sem,
    store_sem,
):
    ctgs, rows, lines = flow.shape
    f32 = jnp.float32
    parts = base.shape[0]
    width = lines // parts
    tiles = width // LANES

    def part(j):
        return pl.ds(j * width, width)

    pairs = [
        (outage_line_in, outage_line),
        (step_in, step_sizes),
        (base_in, base),
        (outage_in, column),
        (limit_in, limit),
        (fresh_in, fresh),
        (balance_in, balance),
        (ramp_in, ramp),
    ]
    loads = [pltpu.make_async_copy(a, b, sem.at[i]) for i, (a, b) in enumerate(pairs)]
    flows = [
        pltpu.make_async_copy(flow_in.at[:, :, part(j)], flow.at[:, :, part(j)], flow_sem.at[j])
        for j in range(parts)
    ]
    for load in loads[:5] + flows + loads[5:]:
        load.start()
    for load in loads[:4]:
        load.wait()
    flow_step = step_sizes[1]
    lane = lax.broadcasted_iota(jnp.int32, (rows, LANES), 1)

    def pick(k, found):
        j = k // tiles
        here = pl.ds(pl.multiple_of((k - j * tiles) * LANES, LANES), LANES)
        block = base[j, :, here]
        return tuple(
            found[c] + jnp.where(lane == outage_line[c] - k * LANES, block, 0.0) for c in range(ctgs)
        )

    zeros = tuple(jnp.zeros((rows, LANES), f32) for c in range(ctgs))
    found = lax.fori_loop(0, lines // LANES, pick, zeros, unroll=4)
    outflow = [flow_step * jnp.sum(f, 1, keepdims=True) for f in found]
    line_of = column_of(outage_line, ctgs, jnp.int32)
    position = lax.broadcasted_iota(jnp.int32, (ctgs, lines), 1)
    column[...] = jnp.where(position == line_of, -1.0, column[...])
    for load in loads[4:]:
        load.wait()
    stores = [
        pltpu.make_async_copy(a, b, store_sem.at[i])
        for i, (a, b) in enumerate([(fresh, fresh_to), (balance, balance_to), (ramp, ramp_to)])
    ]
    for store in stores:
        store.start()

    def update(k, unused):
        j = k // tiles
        here = pl.ds(pl.multiple_of(k * LANES, LANES), LANES)
        inner = pl.ds(pl.multiple_of((k - j * tiles) * LANES, LANES), LANES)
        shared = flow_step * base[j, :, inner]
        bound = flow_step * limit[:, here]
        for c in range(ctgs):
            value = flow[c, :, here] + (shared + column[c : c + 1, here] * outflow[c])
            new_flow[c, :, here] = value - jnp.minimum(jnp.maximum(value, -bound), bound)
        return unused

    for j in range(parts):
        flows[j].wait()
        lax.fori_loop(j * tiles, (j + 1) * tiles, update, 0, unroll=4)
        store = pltpu.make_async_copy(new_flow.at[:, :, part(j)], flow_to.at[:, :, part(j)], store_sem.at[3 + j])
        store.start()
        stores.append(store)
    for store in stores:
        store.wait()


def fused(
    dispatch,
    unit_cost,
    capacity,
    demand,
    balance_dual,
    ramp_dual,
    ramp_band,
    horizon_start,
    shift_factors,
    outage_factors,
    outage_line,
    line_limit,
    flow_dual,
    step_sizes,
):
    f32 = jnp.float32
    rows, own = dispatch.shape
    ctgs, unused, lines = flow_dual.shape
    buses = shift_factors.shape[1]
    line_block = lines // 4
    anywhere = pl.BlockSpec(memory_space=pl.ANY)
    hbm = pl.BlockSpec(memory_space=pltpu.HBM)
    small = jax.ShapeDtypeStruct((rows, own), f32)
    single = jax.ShapeDtypeStruct((1, rows), f32)
    outs = pl.pallas_call(
        functools.partial(kernel, buses),
        out_shape=(small, jax.ShapeDtypeStruct((4, rows, line_block), f32), single, small),
        in_specs=[hbm] * 13,
        out_specs=[anywhere] * 4,
        scratch_shapes=[
            pltpu.SMEM((rows,), f32),
            pltpu.SMEM((rows,), f32),
            pltpu.SMEM((rows,), jnp.int32),
            pltpu.SMEM((ctgs,), jnp.int32),
            pltpu.SMEM((4,), f32),
            pltpu.VMEM((rows, own), f32),
            pltpu.VMEM((1, rows), f32),
            pltpu.VMEM((rows, own), f32),
            pltpu.VMEM((rows, own), f32),
            pltpu.VMEM((rows, own), f32),
            pltpu.VMEM((1, own), f32),
            pltpu.VMEM((rows, own), f32),
            pltpu.VMEM((1, own), jnp.int32),
            pltpu.VMEM(shift_factors.shape, f32),
            pltpu.VMEM(outage_factors.shape, f32),
            pltpu.VMEM(flow_dual.shape, f32),
            pltpu.VMEM(shift_factors.shape, jnp.bfloat16),
            pltpu.VMEM(shift_factors.shape, jnp.bfloat16),
            pltpu.VMEM((rows, lines), f32),
            pltpu.VMEM((3, rows, line_block), f32),
            pltpu.VMEM((3, rows, own), f32),
            pltpu.VMEM((3, rows, own), f32),
            pltpu.VMEM((4, rows, own), f32),
            pltpu.VMEM((4, rows, line_block), f32),
            pltpu.VMEM((1, own), f32),
            pltpu.VMEM((1, own), f32),
            pltpu.VMEM((1, own), f32),
            pltpu.VMEM((1, own), f32),
            pltpu.SemaphoreType.DMA((12,)),
            pltpu.SemaphoreType.DMA((7,)),
            pltpu.SemaphoreType.DMA((8,)),
            pltpu.SemaphoreType.DMA((4, 3)),
            pltpu.SemaphoreType.DMA((4, 3)),
            pltpu.SemaphoreType.DMA((2,)),
            pltpu.SemaphoreType.DMA((2,)),
        ],
        compiler_params=pltpu.CompilerParams(
            collective_id=0, has_side_effects=True, vmem_limit_bytes=61 * 2**20
        ),
    )(
        demand,
        balance_dual,
        horizon_start,
        outage_line,
        step_sizes,
        dispatch,
        unit_cost,
        capacity.reshape(1, own),
        ramp_dual,
        ramp_band.reshape(1, own),
        shift_factors,
        outage_factors,
        flow_dual,
    )
    outs = pl.pallas_call(
        finish,
        out_shape=(small, jax.ShapeDtypeStruct(flow_dual.shape, f32), single, small),
        in_specs=[hbm] * 9,
        out_specs=[hbm] * 4,
        scratch_shapes=[
            pltpu.VMEM((rows, own), f32),
            pltpu.VMEM((4, rows, line_block), f32),
            pltpu.VMEM((1, rows), f32),
            pltpu.VMEM((rows, own), f32),
            pltpu.VMEM(outage_factors.shape, f32),
            pltpu.SMEM((ctgs,), jnp.int32),
            pltpu.VMEM((1, lines), f32),
            pltpu.VMEM(flow_dual.shape, f32),
            pltpu.SMEM((4,), f32),
            pltpu.VMEM(flow_dual.shape, f32),
            pltpu.SemaphoreType.DMA((8,)),
            pltpu.SemaphoreType.DMA((4,)),
            pltpu.SemaphoreType.DMA((7,)),
        ],
        compiler_params=pltpu.CompilerParams(vmem_limit_bytes=61 * 2**20),
    )(*outs, outage_factors, outage_line, line_limit.reshape(1, lines), flow_dual, step_sizes)
    return outs[0], outs[1], outs[2].reshape(rows), outs[3]


def choose(*blocks):
    rows, own = blocks[0].shape
    lines = blocks[9].shape[1]
    whole = rows == 8 and own % LANES == 0 and lines % (4 * LANES) == 0
    if lax.axis_size("ctg") == 4 and lax.axis_size("tm") > 2 and whole:
        return fused(*blocks)
    return local(*blocks)


def solution(mesh):
    in_specs = (
        P(("groups", "tm"), "ctg"),
        P(("groups", "tm"), "ctg"),
        P("ctg"),
        P(("groups", "tm")),
        P(("groups", "tm")),
        P(("groups", "tm"), "ctg"),
        P("ctg"),
        P("tm"),
        P("ctg", None),
        P("ctg", None),
        P("ctg"),
        P(),
        P("ctg", ("groups", "tm"), None),
        P(),
    )
    out_specs = (
        P(("groups", "tm"), "ctg"),
        P("ctg", ("groups", "tm"), None),
        P(("groups", "tm")),
        P(("groups", "tm"), "ctg"),
    )
    return jax.shard_map(choose, mesh=mesh, in_specs=in_specs, out_specs=out_specs, check_vma=False)
```

```python
import functools
import jax
import jax.numpy as jnp
from jax import lax
from jax.experimental import pallas as pl
from jax.experimental.pallas import tpu as pltpu
from jax.sharding import PartitionSpec as P

BUSES = 2048


highest = lax.Precision.HIGHEST


def from_behind(block, axis, distance):
    devices = range(lax.axis_size(axis))
    route = [(i - distance, i) for i in devices if i - distance in devices]
    return lax.ppermute(block, axis, route)


def dual_update(value, step, bound):
    return value - step * jnp.clip(value / step, -bound, bound)


def local(
    dispatch,
    unit_cost,
    capacity,
    demand,
    balance_dual,
    ramp_dual,
    ramp_band,
    horizon_start,
    shift_factors,
    outage_factors,
    outage_line,
    line_limit,
    flow_dual,
    step_sizes,
):
    count_times = dispatch.shape[0]
    total_lines = outage_factors.shape[1]
    primal_step = 0.1 * step_sizes[0]
    flow_step = step_sizes[1]
    balance_step = step_sizes[2] / BUSES
    ramp_step = step_sizes[3]
    first_time = lax.axis_index("tm") * count_times
    times = first_time + jnp.arange(count_times, dtype=jnp.int32)
    coupled = jnp.where((times > 0) & (horizon_start == 0), 1.0, 0.0).astype(jnp.float32)
    ramp_limit = 0.05 * ramp_band.astype(jnp.float32)
    positions = jnp.arange(total_lines, dtype=jnp.int32)
    is_outage = positions[None, :] == outage_line[:, None]
    column = jnp.where(is_outage, -1.0, outage_factors)
    marker = is_outage.astype(jnp.float32)
    product = jnp.einsum("ctl,cl->ct", flow_dual, column, precision=highest)
    adjoint = jnp.sum(flow_dual, 0) + jnp.einsum("ct,cl->tl", product, marker, precision=highest)
    line_part = lax.psum_scatter(adjoint, "ctg", scatter_dimension=1, tiled=True)
    partial_bus = jnp.dot(line_part, shift_factors, precision=highest)
    bus_part = lax.psum_scatter(partial_bus, "ctg", scatter_dimension=1, tiled=True)
    weighted = ramp_dual * coupled[:, None]
    incoming = from_behind(weighted[:1], "tm", -1)
    following = jnp.concatenate([weighted[1:], incoming], 0)
    gradient = unit_cost + balance_dual[:, None] + bus_part + weighted - following
    new_dispatch = jnp.clip(dispatch - primal_step * gradient, 0.0, capacity[None, :])
    extended = 2.0 * new_dispatch - dispatch
    base_mine = jnp.dot(
        lax.all_gather(extended, "ctg", axis=1, tiled=True), shift_factors.T, precision=highest
    )
    total = lax.psum(jnp.sum(extended, 1), "ctg")
    base = lax.all_gather(base_mine, "ctg", axis=1, tiled=True)
    outflow = jnp.einsum("tl,cl->ct", base, marker, precision=highest)
    flow = base[None, :, :] + column[:, None, :] * outflow[:, :, None]
    new_flow_dual = dual_update(flow_dual + flow_step * flow, flow_step, line_limit[None, None, :])
    new_balance_dual = balance_dual + balance_step * (total - demand)
    previous = from_behind(extended[-1:], "tm", 1)
    before = jnp.concatenate([previous, extended[:-1]], 0)
    ramp_value = ramp_dual + ramp_step * (extended - before)
    new_ramp_dual = coupled[:, None] * dual_update(ramp_value, ramp_step, ramp_limit[None, :])
    return (new_dispatch, new_flow_dual, new_balance_dual, new_ramp_dual)


MESH = pl.DeviceIdType.MESH
LANES = 128


def partner(me, k):
    if k == 3:
        return 3 - me
    if k == 2:
        return lax.rem(me + 2, 4)
    return me + 1 - 2 * lax.rem(me, 2)


def column_of(scalars, rows, dtype):
    place = lax.broadcasted_iota(jnp.int32, (rows, 1), 0)
    result = jnp.zeros((rows, 1), dtype)
    for i in range(rows):
        result = jnp.where(place == i, scalars[i], result)
    return result


def split(x):
    high = x.astype(jnp.bfloat16)
    low = (x - high.astype(jnp.float32)).astype(jnp.bfloat16)
    return high, low


def times(x, high, low, axis):
    rows = x.shape[0]
    both = jnp.concatenate(split(x), 0)
    dims = (((1,), (axis,)), ((), ()))
    a = lax.dot_general(both, high, dims, preferred_element_type=jnp.float32)
    b = lax.dot_general(both, low, dims, preferred_element_type=jnp.float32)
    c = a + b
    return c[:rows] + c[rows:]


def kernel(
    buses,
    demand_in,
    balance_in,
    start_in,
    outage_line_in,
    step_in,
    dispatch_in,
    unit_cost_in,
    capacity_in,
    ramp_dual_in,
    ramp_band_in,
    shift_in,
    outage_in,
    flow_in,
    dispatch_to,
    base_to,
    balance_to,
    ramp_to,
    demand,
    balance_dual,
    horizon_start,
    outage_line,
    step_sizes,
    new_dispatch,
    new_balance,
    new_ramp,
    dispatch,
    unit_cost,
    capacity,
    ramp_dual,
    ramp_band,
    shift,
    column,
    flow,
    high,
    low,
    adjoint,
    adjoint_got,
    bus,
    bus_got,
    extended_all,
    base_all,
    row_out,
    row_in,
    last_out,
    last_in,
    load_sem,
    store_sem,
    shift_sem,
    send_sem,
    recv_sem,
    row_send,
    row_recv,
):
    me = lax.axis_index("ctg")
    tm = lax.axis_index("tm")
    tms = lax.axis_size("tm")
    ctgs, rows, lines = flow.shape
    mine_lines = lines // 4
    mine_buses = buses // 4
    f32 = jnp.float32
    after = lax.rem(tm + 1, tms)
    ahead = lax.rem(tm + tms - 1, tms)

    barrier = pltpu.get_barrier_semaphore()
    for k in (2, 3, 1):
        pl.semaphore_signal(barrier, inc=1, device_id={"ctg": partner(me, k)}, device_id_type=MESH)
    for t in (after, ahead):
        pl.semaphore_signal(barrier, inc=1, device_id={"tm": t}, device_id_type=MESH)

    loads = [
        pltpu.make_async_copy(a, b, load_sem.at[i])
        for i, (a, b) in enumerate(
            [
                (flow_in, flow),
                (outage_in, column),
                (ramp_dual_in, ramp_dual),
                (dispatch_in, dispatch),
                (unit_cost_in, unit_cost),
                (capacity_in, capacity),
                (ramp_band_in, ramp_band),
                (outage_line_in, outage_line),
                (step_in, step_sizes),
                (start_in, horizon_start),
                (balance_in, balance_dual),
                (demand_in, demand),
            ]
        )
    ]
    for load in loads:
        load.start()
    pieces = shift_sem.shape[0]
    depth = mine_lines // pieces

    def piece(i):
        there = pl.ds(pl.multiple_of(i * depth, depth), depth)
        return pltpu.make_async_copy(shift_in.at[there], shift.at[there], shift_sem.at[i])

    for i in range(pieces):
        piece(i).start()

    for load in loads[7:]:
        load.wait()
    primal_step = 0.1 * step_sizes[0]
    flow_step = step_sizes[1]
    balance_step = step_sizes[2] / buses
    ramp_step = step_sizes[3]
    starts = column_of(horizon_start, rows, jnp.int32)
    time = tm * rows + lax.broadcasted_iota(jnp.int32, (rows, 1), 0)
    coupled = jnp.where((time > 0) & (starts == 0), 1.0, 0.0).astype(f32)
    balance = column_of(balance_dual, rows, f32)
    lane = lax.broadcasted_iota(jnp.int32, (rows, LANES), 1)
    line_of = column_of(outage_line, ctgs, jnp.int32)

    loads[1].wait()
    position = lax.broadcasted_iota(jnp.int32, (ctgs, lines), 1)
    column[...] = jnp.where(position == line_of, -1.0, column[...])
    loads[0].wait()

    def gather_product(k, sums):
        here = pl.ds(pl.multiple_of(k * LANES, LANES), LANES)
        total = jnp.zeros((rows, LANES), f32)
        result = []
        for c in range(ctgs):
            duals = flow[c, :, here]
            total = total + duals
            result.append(sums[c] + duals * column[c : c + 1, here])
        adjoint[:, here] = total
        return tuple(result)

    zeros = tuple(jnp.zeros((rows, LANES), f32) for c in range(ctgs))
    sums = lax.fori_loop(0, lines // LANES, gather_product, zeros, unroll=4)
    product = [jnp.sum(s, 1, keepdims=True) for s in sums]

    def add_product(k, unused):
        here = pl.ds(pl.multiple_of(k * LANES, LANES), LANES)
        total = adjoint[:, here]
        for c in range(ctgs):
            total = total + jnp.where(lane == outage_line[c] - k * LANES, product[c], 0.0)
        adjoint[:, here] = total
        return unused

    lax.fori_loop(0, lines // LANES, add_product, 0, unroll=4)

    def to_partner(phase, k, source, target):
        return pltpu.make_async_remote_copy(
            src_ref=source,
            dst_ref=target,
            send_sem=send_sem.at[phase, k - 1],
            recv_sem=recv_sem.at[phase, k - 1],
            device_id={"ctg": partner(me, k)},
            device_id_type=MESH,
        )

    def span(i, width):
        return pl.ds(pl.multiple_of(i * width, width), width)

    pl.semaphore_wait(barrier, 5)
    first = {}
    for k in (2, 3, 1):
        first[k] = to_partner(0, k, adjoint.at[:, span(partner(me, k), mine_lines)], adjoint_got.at[k - 1])
        first[k].start()
    loads[2].wait()
    weighted = ramp_dual[...] * coupled
    row_out[...] = weighted[:1]
    row_copy = pltpu.make_async_remote_copy(
        src_ref=row_out, dst_ref=row_in, send_sem=row_send.at[0], recv_sem=row_recv.at[0],
        device_id={"tm": ahead}, device_id_type=MESH)
    row_copy.start()

    @pl.loop(0, pieces)
    def _(i):
        piece(i).wait()

        @pl.loop(0, depth // 16)
        def _(r):
            there = pl.ds(pl.multiple_of(i * depth + r * 16, 16), 16)
            a, b = split(shift[there])
            high[there] = a
            low[there] = b

    for load in loads[3:7]:
        load.wait()

    line_part = adjoint[:, span(me, mine_lines)]
    for k in (1, 2, 3):
        first[k].wait_recv()
        line_part = line_part + adjoint_got[k - 1]

    second = {}
    for k in (3, 2, 1, 0):
        owner = partner(me, k) if k else me
        there = span(owner, mine_buses)
        part = times(line_part, high[:, there], low[:, there], 0)
        if k:
            bus[k - 1] = part
            second[k] = to_partner(1, k, bus.at[k - 1], bus_got.at[k - 1])
            second[k].start()
    bus_part = part
    row_copy.wait_recv()
    sub = lax.broadcasted_iota(jnp.int32, (rows, mine_buses), 0)
    incoming = jnp.where(tm == tms - 1, 0.0, row_in[...])
    following = jnp.where(sub == rows - 1, incoming, jnp.roll(weighted, -1, 0))
    known = unit_cost[...] + balance + weighted - following
    for k in (1, 2, 3):
        second[k].wait_recv()
        bus_part = bus_part + bus_got[k - 1]
    gradient = known + bus_part
    fresh = jnp.minimum(jnp.maximum(dispatch[...] - primal_step * gradient, 0.0), capacity[...])
    extended = 2.0 * fresh - dispatch[...]
    extended_all[me] = extended
    third = {}
    for k in (2, 3, 1):
        third[k] = to_partner(2, k, extended_all.at[me], extended_all.at[me])
        third[k].start()
    last_out[...] = extended[rows - 1 :]
    last_copy = pltpu.make_async_remote_copy(
        src_ref=last_out, dst_ref=last_in, send_sem=row_send.at[1], recv_sem=row_recv.at[1],
        device_id={"tm": after}, device_id_type=MESH)
    last_copy.start()
    new_dispatch[...] = fresh
    stores = [pltpu.make_async_copy(new_dispatch, dispatch_to, store_sem.at[0])]
    stores[0].start()

    base = None
    for k in (0, 1, 2, 3):
        if k:
            third[k].wait_recv()
        owner = partner(me, k) if k else me
        block = extended_all[owner]
        there = span(owner, mine_buses)
        if k < 3:
            part = times(block, high[:, there], low[:, there], 1)
            base = part if base is None else base + part
    half = mine_lines // 2
    fourth = {}
    for h in range(2):
        cut = pl.ds(h * half, half)
        part = times(block, high[cut, there], low[cut, there], 1)
        base_all[me, :, cut] = base[:, h * half : (h + 1) * half] + part
        for k in (2, 3, 1):
            piece_of = base_all.at[me, :, cut]
            fourth[h, k] = to_partner(3 + h, k, piece_of, piece_of)
            fourth[h, k].start()

    total = jnp.sum(extended_all[0] + extended_all[1] + extended_all[2] + extended_all[3], 1, keepdims=True)
    wanted = column_of(demand, rows, f32)
    settled = balance + balance_step * (total - wanted)
    eye = lax.broadcasted_iota(jnp.int32, (rows, rows), 0) == lax.broadcasted_iota(jnp.int32, (rows, rows), 1)
    new_balance[...] = jnp.sum(jnp.where(eye, settled, 0.0), 0, keepdims=True)
    last_copy.wait_recv()
    previous = jnp.where(tm == 0, 0.0, last_in[...])
    before = jnp.where(sub == 0, previous, jnp.roll(extended, 1, 0))
    ramp_value = ramp_dual[...] + ramp_step * (extended - before)
    band = ramp_step * (0.05 * ramp_band[...].astype(f32))
    new_ramp[...] = coupled * (ramp_value - jnp.minimum(jnp.maximum(ramp_value, -band), band))
    stores.append(pltpu.make_async_copy(new_balance, balance_to, store_sem.at[1]))
    stores.append(pltpu.make_async_copy(new_ramp, ramp_to, store_sem.at[2]))
    stores[1].start()
    stores[2].start()

    for k in (0, 1, 2, 3):
        if k:
            fourth[0, k].wait_recv()
            fourth[1, k].wait_recv()
        owner = partner(me, k) if k else me
        stores.append(pltpu.make_async_copy(base_all.at[owner], base_to.at[owner], store_sem.at[3 + k]))
        stores[-1].start()

    for group in (first, second, third, fourth):
        for copy in group.values():
            copy.wait_send()
    row_copy.wait_send()
    last_copy.wait_send()
    for store in stores:
        store.wait()


def finish(
    fresh_in,
    base_in,
    balance_in,
    ramp_in,
    outage_in,
    outage_line_in,
    limit_in,
    flow_in,
    step_in,
    fresh_to,
    flow_to,
    balance_to,
    ramp_to,
    fresh,
    base,
    balance,
    ramp,
    column,
    outage_line,
    limit,
    flow,
    step_sizes,
    new_flow,
    sem,
    flow_sem,
    store_sem,
):
    ctgs, rows, lines = flow.shape
    f32 = jnp.float32
    parts = base.shape[0]
    width = lines // parts
    tiles = width // LANES

    def part(j):
        return pl.ds(j * width, width)

    pairs = [
        (outage_line_in, outage_line),
        (step_in, step_sizes),
        (base_in, base),
        (outage_in, column),
        (limit_in, limit),
        (fresh_in, fresh),
        (balance_in, balance),
        (ramp_in, ramp),
    ]
    loads = [pltpu.make_async_copy(a, b, sem.at[i]) for i, (a, b) in enumerate(pairs)]
    flows = [
        pltpu.make_async_copy(flow_in.at[:, :, part(j)], flow.at[:, :, part(j)], flow_sem.at[j])
        for j in range(parts)
    ]
    for load in loads[:5] + flows + loads[5:]:
        load.start()
    for load in loads[:4]:
        load.wait()
    flow_step = step_sizes[1]
    lane = lax.broadcasted_iota(jnp.int32, (rows, LANES), 1)

    def pick(k, found):
        j = k // tiles
        here = pl.ds(pl.multiple_of((k - j * tiles) * LANES, LANES), LANES)
        block = base[j, :, here]
        return tuple(
            found[c] + jnp.where(lane == outage_line[c] - k * LANES, block, 0.0) for c in range(ctgs)
        )

    zeros = tuple(jnp.zeros((rows, LANES), f32) for c in range(ctgs))
    found = lax.fori_loop(0, lines // LANES, pick, zeros, unroll=4)
    outflow = [flow_step * jnp.sum(f, 1, keepdims=True) for f in found]
    line_of = column_of(outage_line, ctgs, jnp.int32)
    position = lax.broadcasted_iota(jnp.int32, (ctgs, lines), 1)
    column[...] = jnp.where(position == line_of, -1.0, column[...])
    for load in loads[4:]:
        load.wait()
    stores = [
        pltpu.make_async_copy(a, b, store_sem.at[i])
        for i, (a, b) in enumerate([(fresh, fresh_to), (balance, balance_to), (ramp, ramp_to)])
    ]
    for store in stores:
        store.start()

    def update(k, unused):
        j = k // tiles
        here = pl.ds(pl.multiple_of(k * LANES, LANES), LANES)
        inner = pl.ds(pl.multiple_of((k - j * tiles) * LANES, LANES), LANES)
        shared = flow_step * base[j, :, inner]
        bound = flow_step * limit[:, here]
        for c in range(ctgs):
            value = flow[c, :, here] + (shared + column[c : c + 1, here] * outflow[c])
            new_flow[c, :, here] = value - jnp.minimum(jnp.maximum(value, -bound), bound)
        return unused

    for j in range(parts):
        flows[j].wait()
        lax.fori_loop(j * tiles, (j + 1) * tiles, update, 0, unroll=4)
        store = pltpu.make_async_copy(new_flow.at[:, :, part(j)], flow_to.at[:, :, part(j)], store_sem.at[3 + j])
        store.start()
        stores.append(store)
    for store in stores:
        store.wait()


def fused(
    dispatch,
    unit_cost,
    capacity,
    demand,
    balance_dual,
    ramp_dual,
    ramp_band,
    horizon_start,
    shift_factors,
    outage_factors,
    outage_line,
    line_limit,
    flow_dual,
    step_sizes,
):
    f32 = jnp.float32
    rows, own = dispatch.shape
    ctgs, unused, lines = flow_dual.shape
    buses = shift_factors.shape[1]
    line_block = lines // 4
    anywhere = pl.BlockSpec(memory_space=pl.ANY)
    hbm = pl.BlockSpec(memory_space=pltpu.HBM)
    small = jax.ShapeDtypeStruct((rows, own), f32)
    single = jax.ShapeDtypeStruct((1, rows), f32)
    outs = pl.pallas_call(
        functools.partial(kernel, buses),
        out_shape=(small, jax.ShapeDtypeStruct((4, rows, line_block), f32), single, small),
        in_specs=[hbm] * 13,
        out_specs=[anywhere] * 4,
        scratch_shapes=[
            pltpu.SMEM((rows,), f32),
            pltpu.SMEM((rows,), f32),
            pltpu.SMEM((rows,), jnp.int32),
            pltpu.SMEM((ctgs,), jnp.int32),
            pltpu.SMEM((4,), f32),
            pltpu.VMEM((rows, own), f32),
            pltpu.VMEM((1, rows), f32),
            pltpu.VMEM((rows, own), f32),
            pltpu.VMEM((rows, own), f32),
            pltpu.VMEM((rows, own), f32),
            pltpu.VMEM((1, own), f32),
            pltpu.VMEM((rows, own), f32),
            pltpu.VMEM((1, own), jnp.int32),
            pltpu.VMEM(shift_factors.shape, f32),
            pltpu.VMEM(outage_factors.shape, f32),
            pltpu.VMEM(flow_dual.shape, f32),
            pltpu.VMEM(shift_factors.shape, jnp.bfloat16),
            pltpu.VMEM(shift_factors.shape, jnp.bfloat16),
            pltpu.VMEM((rows, lines), f32),
            pltpu.VMEM((3, rows, line_block), f32),
            pltpu.VMEM((3, rows, own), f32),
            pltpu.VMEM((3, rows, own), f32),
            pltpu.VMEM((4, rows, own), f32),
            pltpu.VMEM((4, rows, line_block), f32),
            pltpu.VMEM((1, own), f32),
            pltpu.VMEM((1, own), f32),
            pltpu.VMEM((1, own), f32),
            pltpu.VMEM((1, own), f32),
            pltpu.SemaphoreType.DMA((12,)),
            pltpu.SemaphoreType.DMA((7,)),
            pltpu.SemaphoreType.DMA((8,)),
            pltpu.SemaphoreType.DMA((5, 3)),
            pltpu.SemaphoreType.DMA((5, 3)),
            pltpu.SemaphoreType.DMA((2,)),
            pltpu.SemaphoreType.DMA((2,)),
        ],
        compiler_params=pltpu.CompilerParams(
            collective_id=0, has_side_effects=True, vmem_limit_bytes=61 * 2**20
        ),
    )(
        demand,
        balance_dual,
        horizon_start,
        outage_line,
        step_sizes,
        dispatch,
        unit_cost,
        capacity.reshape(1, own),
        ramp_dual,
        ramp_band.reshape(1, own),
        shift_factors,
        outage_factors,
        flow_dual,
    )
    outs = pl.pallas_call(
        finish,
        out_shape=(small, jax.ShapeDtypeStruct(flow_dual.shape, f32), single, small),
        in_specs=[hbm] * 9,
        out_specs=[hbm] * 4,
        scratch_shapes=[
            pltpu.VMEM((rows, own), f32),
            pltpu.VMEM((4, rows, line_block), f32),
            pltpu.VMEM((1, rows), f32),
            pltpu.VMEM((rows, own), f32),
            pltpu.VMEM(outage_factors.shape, f32),
            pltpu.SMEM((ctgs,), jnp.int32),
            pltpu.VMEM((1, lines), f32),
            pltpu.VMEM(flow_dual.shape, f32),
            pltpu.SMEM((4,), f32),
            pltpu.VMEM(flow_dual.shape, f32),
            pltpu.SemaphoreType.DMA((8,)),
            pltpu.SemaphoreType.DMA((4,)),
            pltpu.SemaphoreType.DMA((7,)),
        ],
        compiler_params=pltpu.CompilerParams(vmem_limit_bytes=61 * 2**20),
    )(*outs, outage_factors, outage_line, line_limit.reshape(1, lines), flow_dual, step_sizes)
    return outs[0], outs[1], outs[2].reshape(rows), outs[3]


def choose(*blocks):
    rows, own = blocks[0].shape
    lines = blocks[9].shape[1]
    whole = rows == 8 and own % LANES == 0 and lines % (8 * LANES) == 0
    if lax.axis_size("ctg") == 4 and lax.axis_size("tm") > 2 and whole:
        return fused(*blocks)
    return local(*blocks)


def solution(mesh):
    in_specs = (
        P(("groups", "tm"), "ctg"),
        P(("groups", "tm"), "ctg"),
        P("ctg"),
        P(("groups", "tm")),
        P(("groups", "tm")),
        P(("groups", "tm"), "ctg"),
        P("ctg"),
        P("tm"),
        P("ctg", None),
        P("ctg", None),
        P("ctg"),
        P(),
        P("ctg", ("groups", "tm"), None),
        P(),
    )
    out_specs = (
        P(("groups", "tm"), "ctg"),
        P("ctg", ("groups", "tm"), None),
        P(("groups", "tm")),
        P(("groups", "tm"), "ctg"),
    )
    return jax.shard_map(choose, mesh=mesh, in_specs=in_specs, out_specs=out_specs, check_vma=False)
```
